32 devices in a mesh: los: 16 (over z, y, core), tr: 2 (over x).
Axes of the slice: x: 2, y: 2, z: 4, core: 2. Of those that a mesh axis runs over, the one named last changes fastest.
Arguments:
- density: bfloat16 [256, 2304], P('los', 'tr'), may hold values from -6 to 6
- observed_counts: int32 [256, 2304], P('los', 'tr'), may hold values from 0 to 5
- cell_targets: int32 [256, 2304], P('los', 'tr'), may hold values from 0 to 127
- shift_bins: int32 [256, 18], P('los', 'tr'), may hold values from -111 to 111, as said below
- kernel_first: bfloat16 [27, 32], replicated, may hold values from -1.25 to 1.25
- kernel_second: bfloat16 [864, 32], replicated, may hold values from -0.21875 to 0.21875
- kernel_third: bfloat16 [864, 1], replicated, may hold values from -0.21875 to 0.21875
Outputs:
- redshift_rate: float32 [256, 2304], P('los', 'tr')
- loss: float32 [], replicated
- grad_first: float32 [27, 32], replicated
- grad_second: float32 [864, 32], replicated
- grad_third: float32 [864, 1], replicated
The draws below stay inside these ranges and needn't reach their ends.
Inputs may be any that keep to these rules, and one draw needn't show every extreme that they name: Take blocks of 16 line-of-sight cells and one half of each plane's tiles along the first transverse dimension (tiles 9 b to 9 b + 8). For a tile at cell l of its block, floor((l + shift_bins) / 16) lies in -6..6: the destination block, counted around the loop. Of one block's 144 tiles at most 24 share a destination block, and exactly 24 do for some destination block of every block.
All inputs are finite; a program needn't handle non-finite values.
Results may differ from the reference program's by a relative error of at most 0.00087.
Values may be sent and summed in bfloat16 or wider, within the bound.
A program may use at most 320 MiB of HBM per device.

```python
import jax
import jax.numpy as jnp
from jax import lax

CL = 16
NY = 48
NZ = 48
HID = 32
REACH = 6
NL = 256
TROW = 18
TDEV = 9
TILES_DEV = 144
CAP = 24
NCELLS = 589824


def draw_shift_bins(key, part):
    line_blocks = NL // CL
    plane_blocks = TROW // TDEV
    block_keys = jax.random.split(key, line_blocks * plane_blocks)

    def one_block(block_key):
        first_key, second_key, third_key = jax.random.split(block_key, 3)
        ranking = jax.random.permutation(first_key, TILES_DEV)
        rotation = jax.random.randint(second_key, (), 0, 2 * REACH + 1)
        distance = (ranking // CAP + rotation) % (2 * REACH + 1) - REACH
        landing = jax.random.randint(third_key, (TILES_DEV,), 0, CL)
        source_line = jnp.arange(TILES_DEV) // TDEV
        return (distance * CL + landing - source_line).reshape(CL, TDEV)
    blocks = jax.vmap(one_block)(block_keys).reshape(line_blocks, plane_blocks, CL, TDEV)
    return blocks.transpose(0, 2, 1, 3).reshape(NL, TROW).astype(jnp.int32)


def place_ends(values, key, least, top_value):
    longest = values.shape.index(max(values.shape))
    spots = []
    for shift in (0, 1):
        where = [jax.random.randint(jax.random.fold_in(key, axis), (), 0, length) for axis, length in enumerate(values.shape)]
        where[longest] = (where[longest] + shift) % values.shape[longest]
        spots.append(tuple(where))
    return values.at[spots[0]].set(least).at[spots[1]].set(top_value)


def block_levels(stream_key, dims, shards, smallest, largest):
    loudness, own = 1.0, jax.random.fold_in(stream_key, 6)
    for axis_at, blocks in shards:
        steps = jnp.exp(jax.random.uniform(jax.random.fold_in(own, axis_at), (blocks,), jnp.float32, smallest / len(shards), largest / len(shards)))
        loudness = loudness * jnp.repeat(steps, dims[axis_at] // blocks).reshape([-1 if axis == axis_at else 1 for axis in range(len(dims))])
    return loudness


def normal_values(key, shape, scale, most, cuts=(), kind=jnp.bfloat16):
    gain = block_levels(key, shape, cuts, -0.22, 0.18) if cuts else 1.0
    entries = jax.random.normal(key, shape, jnp.float32) * scale * gain
    return jnp.minimum(jnp.maximum(entries, -most), most).astype(kind)


def setup_inputs(seed: int = 0) -> dict:
    splits = jax.random.split(jax.random.key(seed), 8)
    density = normal_values(splits[0], (NL, NY * NZ), 1.0, 6.0, ((0, 16), (1, 2)))
    observed_counts = place_ends(jax.random.randint(splits[1], (NL, NY * NZ), 0, 6), jax.random.fold_in(splits[1], 1), 0, 5).astype(jnp.int32)
    cell_targets = place_ends(jax.random.randint(splits[2], (NL, NY * NZ), 0, 128), jax.random.fold_in(splits[2], 1), 0, 127).astype(jnp.int32)
    shift_bins = draw_shift_bins(jax.random.fold_in(splits[7], 71), 0)
    kernel_first = normal_values(splits[4], (27, HID), 27 ** -0.5, 1.25)
    kernel_second = normal_values(splits[5], (27 * HID, HID), (27 * HID) ** -0.5, 0.21875)
    kernel_third = normal_values(splits[6], (27 * HID, 1), (27 * HID) ** -0.5, 0.21875)
    return {"density": density, "observed_counts": observed_counts, "cell_targets": cell_targets, "shift_bins": shift_bins, "kernel_first": kernel_first, "kernel_second": kernel_second, "kernel_third": kernel_third}


background = 0.2

def pad_field(field):
    wrapped = jnp.concatenate([field[-1:], field, field[:1]], axis=0)
    return jnp.pad(wrapped, ((0, 0), (1, 1), (1, 1), (0, 0)))

def apply_conv(field, weights):
    padded = pad_field(field.astype(jnp.float32))
    result = lax.conv_general_dilated(padded[None], weights, (1, 1, 1), 'VALID', dimension_numbers=('NDHWC', 'DHWIO', 'NDHWC'), precision=lax.Precision.HIGHEST)
    return result[0]

def convolve(field, kernel, inputs, outputs):
    weights = kernel.astype(jnp.float32).reshape(3, 3, 3, inputs, outputs)
    return apply_conv(field, weights)

def transpose_conv(grad, kernel, inputs, outputs):
    weights = kernel.astype(jnp.float32).reshape(3, 3, 3, inputs, outputs)[::-1, ::-1, ::-1].transpose(0, 1, 2, 4, 3)
    return apply_conv(grad, weights)

def kernel_grad(field, grad, inputs, outputs):
    padded = pad_field(field.astype(jnp.float32))
    extent = grad.shape
    flat_grad = grad.astype(jnp.float32).reshape(-1, outputs)

    def one_tap(tap_index):
        shift_x = tap_index // 9
        shift_y = tap_index // 3 % 3
        shift_z = tap_index % 3
        zero_start = jnp.zeros((), jnp.int32)
        piece = lax.dynamic_slice(padded, (shift_x, shift_y, shift_z, zero_start), (extent[0], extent[1], extent[2], inputs))
        return jnp.dot(piece.reshape(-1, inputs).T, flat_grad, precision=lax.Precision.HIGHEST)
    return lax.map(one_tap, jnp.arange(27, dtype=jnp.int32)).reshape(27 * inputs, outputs)

def silu_slope(value):
    sigmoid = jax.nn.sigmoid(value)
    return sigmoid * (1.0 + value * (1.0 - sigmoid))

def reference(density, observed_counts, cell_targets, shift_bins, kernel_first, kernel_second, kernel_third):
    field = density.reshape(NL, NY, NZ, 1)
    pre_first = convolve(field, kernel_first, 1, HID)
    hidden_first = jax.nn.silu(pre_first).astype(jnp.bfloat16)
    pre_second = convolve(hidden_first, kernel_second, HID, HID)
    hidden_second = jax.nn.silu(pre_second).astype(jnp.bfloat16)
    log_rate = convolve(hidden_second, kernel_third, HID, 1)[..., 0]
    rate = jnp.exp(log_rate).reshape(NL, TROW, 128)
    targets = cell_targets.reshape(NL, TROW, 128)
    line_index = jnp.arange(NL, dtype=jnp.int32)[:, None, None]
    tile_index = jnp.arange(TROW, dtype=jnp.int32)[None, :, None]
    permuted = jnp.zeros((NL, TROW, 128), jnp.float32).at[line_index, tile_index, targets].add(rate)
    landing = (jnp.arange(NL, dtype=jnp.int32)[:, None] + shift_bins) % NL
    tile_column = jnp.arange(TROW, dtype=jnp.int32)[None, :]
    shifted = jnp.zeros((NL, TROW, 128), jnp.float32).at[landing, tile_column].add(permuted)
    redshift_rate = background + shifted
    counts = observed_counts.reshape(NL, TROW, 128).astype(jnp.float32)
    loss = jnp.sum(redshift_rate - counts * jnp.log(redshift_rate)) / NCELLS
    lam_grad = (1.0 - counts / redshift_rate) / NCELLS
    permuted_grad = lam_grad[landing, tile_column]
    rate_grad = jnp.take_along_axis(permuted_grad, targets, axis=2)
    log_grad = (rate_grad * rate).reshape(NL, NY, NZ, 1).astype(jnp.bfloat16)
    grad_third = kernel_grad(hidden_second, log_grad, HID, 1)
    second_back = transpose_conv(log_grad, kernel_third, HID, 1)
    act_second = (second_back * silu_slope(pre_second)).astype(jnp.bfloat16)
    grad_second = kernel_grad(hidden_first, act_second, HID, HID)
    first_back = transpose_conv(act_second, kernel_second, HID, HID)
    act_first = (first_back * silu_slope(pre_first)).astype(jnp.bfloat16)
    grad_first = kernel_grad(field, act_first, 1, HID)
    return (redshift_rate.reshape(NL, NY * NZ), loss, grad_first, grad_second, grad_third)
```

```python
import functools

import jax
import jax.numpy as jnp
from jax import lax
from jax.experimental import pallas as pl
from jax.experimental.pallas import tpu as pltpu
from jax.sharding import PartitionSpec as P

NZ = 48
REACH = 6
SPREAD = 2 * REACH + 1
CAP = 24
PITCH = 32
SLOTS = SPREAD * PITCH
HID = 32
YP = 32
OFF = 4
LANES = NZ * HID
PAD = 128
WIDE = LANES + 2 * PAD
GROUP = 256
GROUPS = LANES // GROUP
BACKGROUND = 0.2
MESH = pl.DeviceIdType.MESH
HIGH = lax.Precision.HIGHEST
LIMIT = 56 * 1024 * 1024
F32 = jnp.float32
BF16 = jnp.bfloat16
NT = (((1,), (1,)), ((), ()))
TN = (((0,), (0,)), ((), ()))


def iota(shape, dim):
    return lax.broadcasted_iota(jnp.int32, shape, dim)


def repeat_lanes(kernel, width):
    rep = jnp.where((iota((HID, width), 1) & (HID - 1)) == iota((HID, width), 0), 1.0, 0.0)
    return jnp.dot(kernel, rep.astype(BF16), preferred_element_type=F32)


def fill_thin_band(kernel, out_ref, flip):
    tiled = repeat_lanes(kernel, LANES)
    diff = iota((NZ, LANES), 0) - (iota((NZ, LANES), 1) >> 5)
    if flip:
        diff = -diff
    for ab in range(9):
        block = jnp.zeros((NZ, LANES), F32)
        for c in range(3):
            row = 3 * ab + c
            block = jnp.where(diff == c - 1, tiled[row : row + 1, :], block)
        out_ref[ab * NZ : (ab + 1) * NZ, :] = block.astype(BF16)


def fill_wide_band(kernel, out_ref):
    tiled = repeat_lanes(kernel, GROUP)
    zo = iota((HID, GROUP), 1) >> 5
    for ab in range(9):
        for zi in range(16):
            block = jnp.zeros((HID, GROUP), F32)
            for c in range(3):
                if 0 <= zi - 3 - c < 8:
                    row = (3 * ab + c) * HID
                    block = jnp.where(zo == zi - 3 - c, tiled[row : row + HID, :], block)
            out_ref[ab, zi * HID : (zi + 1) * HID, :] = block.astype(BF16)


def fill_taps(src_ref, out_ref, lines):
    for ab in range(9):
        a, b = ab // 3, ab % 3
        out_ref[:, :, ab * NZ : (ab + 1) * NZ] = src_ref[a : a + lines, b : b + YP, :]


def y_masks(rows_y, lines, width):
    index = iota((lines, YP, width), 1) - OFF
    start = lax.axis_index("tr") * rows_y
    total = lax.axis_size("tr") * rows_y
    inside = (index + start >= 0) & (index + start < total)
    owned = (index >= 0) & (index < rows_y)
    return inside, owned


def sigmoid(v):
    return 1.0 / (1.0 + jnp.exp(-v))


def slope(v):
    s = sigmoid(v)
    return s * (1.0 + v * (1.0 - s))


def store_shifted(out_ref, g, value):
    lanes = pl.ds(pl.multiple_of(PAD + g * GROUP, 128), GROUP)
    out_ref[0, :, :, lanes] = pltpu.roll(value, 1, 1).astype(BF16)
    out_ref[1, :, :, lanes] = value.astype(BF16)
    out_ref[2, :, :, lanes] = pltpu.roll(value, YP - 1, 1).astype(BF16)


def clear_pads(out_ref):
    shape = out_ref.shape[:-1] + (PAD,)
    out_ref[:, :, :, 0:PAD] = jnp.zeros(shape, BF16)
    out_ref[:, :, :, WIDE - PAD : WIDE] = jnp.zeros(shape, BF16)


def wide_conv(src_ref, band_ref, g, lines):
    total = jnp.zeros((lines * YP, GROUP), F32)
    lanes = pl.ds(pl.multiple_of(g * GROUP, 128), 2 * GROUP)
    for ab in range(9):
        a, b = ab // 3, ab % 3
        block = src_ref[b, a : a + lines, :, lanes].reshape(lines * YP, 2 * GROUP)
        total = total + jnp.dot(block, band_ref[ab], preferred_element_type=F32)
    return total


def forward_kernel(
    lines, rows_y, field_ref, k1_ref, k2_ref, k3_ref,
    rate_ref, pre1_ref, pre2_ref, h1_ref, h2_ref, taps_ref,
    d9, w1, w2, w3, h1b, h2, z9,
):
    l2, l1 = lines + 4, lines + 2
    fill_thin_band(k1_ref[...], w1, False)
    fill_wide_band(k2_ref[...], w2)
    fill_thin_band(k3_ref[...], w3, True)
    fill_taps(field_ref, d9, l2)
    taps_ref[...] = d9[2 : 2 + lines].reshape(lines * YP, 9 * NZ).astype(BF16)
    clear_pads(h1b)

    @pl.loop(0, GROUPS)
    def _(g):
        lanes = pl.ds(pl.multiple_of(g * GROUP, 128), GROUP)
        taps = d9[...].reshape(l2 * YP, 9 * NZ).astype(BF16)
        pre = jnp.dot(taps, w1[:, lanes], preferred_element_type=F32)
        pre = pre.reshape(l2, YP, GROUP)
        pre1_ref[:, :, lanes] = pre[2 : 2 + lines]
        inside, _ = y_masks(rows_y, l2, GROUP)
        _, owned = y_masks(rows_y, lines, GROUP)
        value = jnp.where(inside, pre * sigmoid(pre), 0.0)
        h1_ref[:, :, lanes] = jnp.where(owned, value[2 : 2 + lines], 0.0).astype(BF16)
        store_shifted(h1b, g, value)

    @pl.loop(0, GROUPS)
    def _(g):
        lanes = pl.ds(pl.multiple_of(g * GROUP, 128), GROUP)
        pre = wide_conv(h1b, w2, g, l1).reshape(l1, YP, GROUP)
        pre2_ref[:, :, lanes] = pre
        inside, _ = y_masks(rows_y, l1, GROUP)
        _, owned = y_masks(rows_y, lines, GROUP)
        value = jnp.where(inside, pre * sigmoid(pre), 0.0)
        h2[:, :, lanes] = value.astype(BF16)
        h2_ref[:, :, lanes] = jnp.where(owned, value[1 : 1 + lines], 0.0).astype(BF16)

    z9[...] = lax.dot_general(
        h2[...].reshape(l1 * YP, LANES), w3[...], NT, preferred_element_type=F32
    ).reshape(l1, YP, 9 * NZ)
    total = jnp.zeros((lines, rows_y, NZ), F32)
    for ab in range(9):
        a, b = ab // 3, ab % 3
        row = OFF - 1 + b
        total = total + z9[a : a + lines, row : row + rows_y, ab * NZ : (ab + 1) * NZ]
    rate_ref[...] = jnp.exp(total)


def tile_kernel(
    total_cells, rate_ref, target_ref, count_ref, slot_ref, land_ref,
    red_ref, loss_ref, grad_ref,
    msg, recv, back, ret, marks, send_sem, recv_sem, send_back, recv_back,
):
    tiles = rate_ref.shape[0]
    me, other = lax.axis_index("los"), lax.axis_index("tr")
    size = lax.axis_size("los")

    def peer(distance):
        return (lax.rem(me + distance + size, size), other)

    distances = [d for d in range(SPREAD) if d != REACH]
    barrier = pltpu.get_barrier_semaphore()
    for d in distances:
        pl.semaphore_signal(barrier, inc=1, device_id=peer(d - REACH), device_id_type=MESH)

    def add_tile(t, perm):
        hit = iota((128, 128), 0) == target_ref[pl.ds(t, 1), :]
        column = jnp.sum(jnp.where(hit, rate_ref[pl.ds(t, 1), :], 0.0), axis=1, keepdims=True)
        return jnp.where(iota((128, tiles), 1) == t, column, perm)

    perm = lax.fori_loop(0, tiles, add_tile, jnp.zeros((128, tiles), F32), unroll=4)
    pick = jnp.where(iota((SLOTS, tiles), 0) == slot_ref[...], 1.0, 0.0)
    sent = lax.dot_general(pick, perm, NT, precision=HIGH, preferred_element_type=F32)
    sent = sent.reshape(SPREAD, PITCH, 128)
    landing = land_ref[...].reshape(SPREAD, 1, 128)
    msg[...] = jnp.where(iota((SPREAD, PITCH, 128), 1) == CAP, landing, sent)

    pl.semaphore_wait(barrier, len(distances))
    copies = []
    for d in distances:
        copy = pltpu.make_async_remote_copy(
            src_ref=msg.at[d], dst_ref=recv.at[d],
            send_sem=send_sem.at[d], recv_sem=recv_sem.at[d],
            device_id=peer(d - REACH), device_id_type=MESH,
        )
        copy.start()
        copies.append(copy)
    recv[REACH] = msg[REACH]
    for copy in copies:
        copy.wait_recv()
    for d in range(SPREAD):
        marks[0:1, d * PITCH : (d + 1) * PITCH] = recv[d, CAP : CAP + 1, 0:PITCH]
    place = jnp.where(
        iota((tiles, SLOTS), 0).astype(F32) == marks[0:1, 0:SLOTS], 1.0, 0.0
    )
    arrived = jnp.dot(
        place, recv[...].reshape(SLOTS, 128), precision=HIGH, preferred_element_type=F32
    )
    rate = BACKGROUND + arrived
    red_ref[...] = rate
    counts = count_ref[...].astype(F32)
    lam = (1.0 - counts / rate) / total_cells
    back[...] = lax.dot_general(
        place, lam, TN, precision=HIGH, preferred_element_type=F32
    ).reshape(SPREAD, PITCH, 128)
    returns = []
    for d in distances:
        copy = pltpu.make_async_remote_copy(
            src_ref=back.at[d], dst_ref=ret.at[d],
            send_sem=send_back.at[d], recv_sem=recv_back.at[d],
            device_id=peer(REACH - d), device_id_type=MESH,
        )
        copy.start()
        returns.append(copy)
    ret[REACH] = back[REACH]
    loss_ref[...] = jnp.sum(rate - counts * jnp.log(rate), axis=0, keepdims=True) / total_cells
    for copy in returns:
        copy.wait_recv()
    moved = lax.dot_general(
        pick, ret[...].reshape(SLOTS, 128), TN, precision=HIGH, preferred_element_type=F32
    )
    picked = jnp.take_along_axis(moved, target_ref[...], axis=1)
    grad_ref[...] = (picked * rate_ref[...]).astype(BF16)
    for copy in copies + returns:
        copy.wait_send()


def thin_extract(product, fold):
    diff = iota((NZ, LANES), 0) - (iota((NZ, LANES), 1) >> 5)
    rows = []
    for ab in range(9):
        block = product[ab * NZ : (ab + 1) * NZ, :]
        for c in range(3):
            rows.append(
                jnp.sum(jnp.where(diff == c - 1, block, 0.0), axis=0, keepdims=True)
            )
    rows = jnp.concatenate(rows + [jnp.zeros((5, LANES), F32)], axis=0)
    return jnp.dot(rows, fold, precision=HIGH, preferred_element_type=F32)


def fold_matrix(width):
    return jnp.where((iota((width, HID), 0) & (HID - 1)) == iota((width, HID), 1), 1.0, 0.0)


def backward_kernel(
    lines, rows_y, grad_ref, pre1_ref, pre2_ref, h1_ref, h2_ref, taps_ref, k2_ref, k3_ref,
    out_ref,
    g9, w2, w3, a2b, a1, h1t, prod, sums,
):
    l1 = lines + 2
    fill_wide_band(k2_ref[...], w2)
    fill_thin_band(k3_ref[...], w3, False)
    fill_taps(grad_ref, g9, l1)
    clear_pads(a2b)

    @pl.loop(0, GROUPS)
    def _(g):
        lanes = pl.ds(pl.multiple_of(g * GROUP, 128), GROUP)
        taps = g9[...].reshape(l1 * YP, 9 * NZ).astype(BF16)
        grad = jnp.dot(taps, w3[:, lanes], preferred_element_type=F32)
        grad = grad.reshape(l1, YP, GROUP) * slope(pre2_ref[:, :, lanes])
        inside, _ = y_masks(rows_y, l1, GROUP)
        store_shifted(a2b, g, jnp.where(inside, grad, 0.0))
        h1t[g] = h1_ref[:, :, lanes].reshape(lines * YP, GROUP).astype(F32).T.astype(BF16)

    @pl.loop(0, GROUPS)
    def _(g):
        lanes = pl.ds(pl.multiple_of(g * GROUP, 128), GROUP)
        grad = wide_conv(a2b, w2, g, lines).reshape(lines, YP, GROUP)
        grad = grad * slope(pre1_ref[:, :, lanes])
        _, owned = y_masks(rows_y, lines, GROUP)
        a1[:, :, lanes] = jnp.where(owned, grad, 0.0).astype(BF16)

    fold = fold_matrix(LANES)
    prod[...] = lax.dot_general(
        taps_ref[...], a1[...].reshape(lines * YP, LANES), TN, preferred_element_type=F32
    )
    out_ref[27 * HID : 28 * HID, :] = thin_extract(prod, fold)
    prod[...] = lax.dot_general(
        g9[1 : 1 + lines].reshape(lines * YP, 9 * NZ).astype(BF16),
        h2_ref[...].reshape(lines * YP, LANES), TN, preferred_element_type=F32,
    )
    out_ref[28 * HID : 29 * HID, :] = thin_extract(prod, fold)

    lane_z = iota((HID, 2 * GROUP), 1) >> 5
    for ab in range(9):
        a, b = ab // 3, ab % 3
        total = jnp.zeros((GROUP, 2 * GROUP), F32)
        for g in range(GROUPS):
            block = a2b[b, a : a + lines, :, g * GROUP : (g + 2) * GROUP]
            total = total + jnp.dot(
                h1t[g], block.reshape(lines * YP, 2 * GROUP), preferred_element_type=F32
            )
        for c in range(3):
            part = jnp.zeros((HID, 2 * GROUP), F32)
            for z in range(8):
                part = jnp.where(lane_z == z + 3 + c, total[z * HID : (z + 1) * HID, :], part)
            row = (26 - 3 * ab - c) * HID
            sums[row : row + HID, :] = part
    out_ref[0 : 27 * HID, :] = jnp.dot(
        sums[...], fold_matrix(2 * GROUP), precision=HIGH, preferred_element_type=F32
    )


def extended(block, width):
    lines, rows, depth = block.shape
    position = lax.axis_index("tr")
    size = lax.axis_size("los")
    send = jnp.where(position == 0, block[:, rows - width :], block[:, :width])
    got = lax.ppermute(send, "tr", [(0, 1), (1, 0)])
    none = jnp.zeros_like(got)
    gap = OFF + 1 - width
    low = jnp.where(position == 1, got, none)
    high = jnp.where(position == 0, got, none)
    wide = jnp.concatenate([low, block, high], axis=1)
    wide = jnp.pad(wide, ((0, 0), (gap, YP + 2 - gap - rows - 2 * width), (0, 0)))
    up = [(i, (i + 1) % size) for i in range(size)]
    down = [(j, i) for i, j in up]
    before = lax.ppermute(wide[lines - width :], "los", up)
    after = lax.ppermute(wide[:width], "los", down)
    return jnp.concatenate([before, wide, after], axis=0).astype(F32)


def on_device(
    density, observed_counts, cell_targets, shift_bins, kernel_first, kernel_second, kernel_third
):
    lines, width_tiles = shift_bins.shape
    plane = density.shape[1]
    rows_y = plane // NZ
    tiles = lines * width_tiles
    total_cells = lines * lax.axis_size("los") * plane * lax.axis_size("tr")
    l1, l2 = lines + 2, lines + 4
    vmem = pl.BlockSpec(memory_space=pltpu.VMEM)
    third = kernel_third.reshape(27, HID)
    second_back = kernel_second.reshape(27, HID, HID)[::-1].transpose(0, 2, 1).reshape(-1, HID)

    line = jnp.arange(lines, dtype=jnp.int32)[:, None]
    tile = jnp.arange(width_tiles, dtype=jnp.int32)[None, :]
    reach_line = line + shift_bins
    step = jnp.floor_divide(reach_line, lines)
    landing = ((reach_line - step * lines) * width_tiles + tile).reshape(-1)
    step = (step + REACH).reshape(-1)
    order = jnp.arange(tiles)
    earlier = (step[:, None] == step[None, :]) & (order[:, None] < order[None, :])
    rank = jnp.sum(earlier.astype(jnp.int32), axis=0)
    slot = step * PITCH + rank
    marks = jnp.sum(
        jnp.where(slot[:, None] == jnp.arange(SLOTS)[None, :], landing[:, None] + 1, 0), axis=0
    ) - 1
    marks = jnp.pad(
        marks.astype(F32).reshape(SPREAD, PITCH), ((0, 0), (0, 128 - PITCH)), constant_values=-1.0
    )

    field = extended(density.reshape(lines, rows_y, NZ), 3)
    rate, pre1, pre2, h1, h2, taps = pl.pallas_call(
        functools.partial(forward_kernel, lines, rows_y),
        out_shape=[
            jax.ShapeDtypeStruct((lines, rows_y, NZ), F32),
            jax.ShapeDtypeStruct((lines, YP, LANES), F32),
            jax.ShapeDtypeStruct((l1, YP, LANES), F32),
            jax.ShapeDtypeStruct((lines, YP, LANES), BF16),
            jax.ShapeDtypeStruct((lines, YP, LANES), BF16),
            jax.ShapeDtypeStruct((lines * YP, 9 * NZ), BF16),
        ],
        in_specs=[vmem] * 4,
        out_specs=[vmem] * 6,
        scratch_shapes=[
            pltpu.VMEM((l2, YP, 9 * NZ), F32),
            pltpu.VMEM((9 * NZ, LANES), BF16),
            pltpu.VMEM((9, 2 * GROUP, GROUP), BF16),
            pltpu.VMEM((9 * NZ, LANES), BF16),
            pltpu.VMEM((3, l2, YP, WIDE), BF16),
            pltpu.VMEM((l1, YP, LANES), BF16),
            pltpu.VMEM((l1, YP, 9 * NZ), F32),
        ],
        compiler_params=pltpu.CompilerParams(vmem_limit_bytes=LIMIT),
        name="forward",
    )(field, kernel_first, kernel_second, third)

    box = pltpu.VMEM((SPREAD, PITCH, 128), F32)
    sems = pltpu.SemaphoreType.DMA((SPREAD,))
    redshift_rate, loss_part, log_grad = pl.pallas_call(
        functools.partial(tile_kernel, total_cells),
        out_shape=[
            jax.ShapeDtypeStruct((tiles, 128), F32),
            jax.ShapeDtypeStruct((1, 128), F32),
            jax.ShapeDtypeStruct((tiles, 128), BF16),
        ],
        in_specs=[vmem] * 5,
        out_specs=[vmem] * 3,
        scratch_shapes=[box, box, box, box, pltpu.VMEM((8, 512), F32), sems, sems, sems, sems],
        compiler_params=pltpu.CompilerParams(
            vmem_limit_bytes=LIMIT, collective_id=0, has_side_effects=True
        ),
        name="tiles",
    )(
        rate.reshape(tiles, 128),
        cell_targets.reshape(tiles, 128),
        observed_counts.reshape(tiles, 128),
        slot.reshape(1, tiles),
        marks,
    )

    grad = extended(log_grad.reshape(lines, rows_y, NZ), 2)
    packed = pl.pallas_call(
        functools.partial(backward_kernel, lines, rows_y),
        out_shape=jax.ShapeDtypeStruct((29 * HID, HID), F32),
        in_specs=[vmem] * 8,
        out_specs=vmem,
        scratch_shapes=[
            pltpu.VMEM((l1, YP, 9 * NZ), F32),
            pltpu.VMEM((9, 2 * GROUP, GROUP), BF16),
            pltpu.VMEM((9 * NZ, LANES), BF16),
            pltpu.VMEM((3, l1, YP, WIDE), BF16),
            pltpu.VMEM((lines, YP, LANES), BF16),
            pltpu.VMEM((GROUPS, GROUP, lines * YP), BF16),
            pltpu.VMEM((9 * NZ, LANES), F32),
            pltpu.VMEM((27 * HID, 2 * GROUP), F32),
        ],
        compiler_params=pltpu.CompilerParams(vmem_limit_bytes=LIMIT),
        name="backward",
    )(grad, pre1, pre2, h1, h2, taps, second_back, third[::-1])
    packed = packed.at[29 * HID - 1, 0].set(jnp.sum(loss_part))
    packed = lax.psum(packed, ("los", "tr"))
    return (
        redshift_rate.reshape(lines, plane),
        packed[29 * HID - 1, 0],
        packed[27 * HID : 27 * HID + 27],
        packed[: 27 * HID],
        packed[28 * HID : 28 * HID + 27][::-1].reshape(27 * HID, 1),
    )


def solution(mesh):
    return jax.shard_map(
        on_device,
        mesh=mesh,
        in_specs=(P("los", "tr"), P("los", "tr"), P("los", "tr"), P("los", "tr"), P(), P(), P()),
        out_specs=(P("los", "tr"), P(), P(), P(), P()),
        check_vma=False,
    )
```

```python
import functools

import jax
import jax.numpy as jnp
from jax import lax
from jax.experimental import pallas as pl
from jax.experimental.pallas import tpu as pltpu
from jax.sharding import PartitionSpec as P

NZ = 48
REACH = 6
SPREAD = 2 * REACH + 1
CAP = 24
EDGE = 24
SHARDS = 16
SHARD = 16
PITCH = 32
SLOTS = SPREAD * PITCH
HID = 32
PACK = 29 * HID // 4
YP = 32
OFF = 4
LANES = NZ * HID
PAD = 128
WIDE = LANES + 2 * PAD
GROUP = 256
GROUPS = LANES // GROUP
BACKGROUND = 0.2
MESH = pl.DeviceIdType.MESH
HIGH = lax.Precision.HIGHEST
LIMIT = 56 * 1024 * 1024
F32 = jnp.float32
BF16 = jnp.bfloat16
NT = (((1,), (1,)), ((), ()))
TN = (((0,), (0,)), ((), ()))


def row_pieces():
    pieces = []
    for j in range(8):
        done = 0
        while done < NZ:
            tile, first = divmod(j * NZ + done, 128)
            length = min(NZ - done, 128 - first)
            pieces.append((j, tile, first, done, length))
            done += length
    return pieces


PIECES = row_pieces()


def iota(shape, dim):
    return lax.broadcasted_iota(jnp.int32, shape, dim)


def repeat_lanes(kernel, width):
    rep = jnp.where((iota((HID, width), 1) & (HID - 1)) == iota((HID, width), 0), 1.0, 0.0)
    return jnp.dot(kernel, rep.astype(BF16), preferred_element_type=F32)


def fill_thin_band(kernel, out_ref, flip):
    tiled = repeat_lanes(kernel, LANES)
    diff = iota((NZ, LANES), 0) - (iota((NZ, LANES), 1) >> 5)
    if flip:
        diff = -diff
    for ab in range(9):
        block = jnp.zeros((NZ, LANES), F32)
        for c in range(3):
            row = 3 * ab + c
            block = jnp.where(diff == c - 1, tiled[row : row + 1, :], block)
        out_ref[ab * NZ : (ab + 1) * NZ, :] = block.astype(BF16)


def fill_wide_band(kernel, out_ref):
    tiled = repeat_lanes(kernel, GROUP)
    zo = iota((HID, GROUP), 1) >> 5
    for ab in range(9):
        for zi in range(16):
            block = jnp.zeros((HID, GROUP), F32)
            for c in range(3):
                if 0 <= zi - 3 - c < 8:
                    row = (3 * ab + c) * HID
                    block = jnp.where(zo == zi - 3 - c, tiled[row : row + HID, :], block)
            out_ref[ab, zi * HID : (zi + 1) * HID, :] = block.astype(BF16)


def fill_taps(src_ref, out_ref, lines):
    for ab in range(9):
        a, b = ab // 3, ab % 3
        out_ref[:, :, ab * NZ : (ab + 1) * NZ] = src_ref[a : a + lines, b : b + YP, :]


def y_masks(rows_y, lines, width):
    index = iota((lines, YP, width), 1) - OFF
    start = lax.axis_index("tr") * rows_y
    total = lax.axis_size("tr") * rows_y
    inside = (index + start >= 0) & (index + start < total)
    owned = (index >= 0) & (index < rows_y)
    return inside, owned


def sigmoid(v):
    return 1.0 / (1.0 + jnp.exp(-v))


def slope(v):
    s = sigmoid(v)
    return s * (1.0 + v * (1.0 - s))


def store_shifted(out_ref, g, value):
    lanes = pl.ds(pl.multiple_of(PAD + g * GROUP, 128), GROUP)
    out_ref[0, :, :, lanes] = pltpu.roll(value, 1, 1).astype(BF16)
    out_ref[1, :, :, lanes] = value.astype(BF16)
    out_ref[2, :, :, lanes] = pltpu.roll(value, YP - 1, 1).astype(BF16)


def clear_pads(out_ref):
    shape = out_ref.shape[:-1] + (PAD,)
    out_ref[:, :, :, 0:PAD] = jnp.zeros(shape, BF16)
    out_ref[:, :, :, WIDE - PAD : WIDE] = jnp.zeros(shape, BF16)


def wide_conv(src_ref, band_ref, g, lines):
    total = jnp.zeros((lines * YP, GROUP), F32)
    lanes = pl.ds(pl.multiple_of(g * GROUP, 128), 2 * GROUP)
    for ab in range(9):
        a, b = ab // 3, ab % 3
        block = src_ref[b, a : a + lines, :, lanes].reshape(lines * YP, 2 * GROUP)
        total = total + jnp.dot(block, band_ref[ab], preferred_element_type=F32)
    return total


def join_rows(out_ref, own, after, before):
    rows = own.shape[1]
    position = lax.axis_index("tr")
    low = before[:, 8 - OFF - 1 :]
    high = after[:, : YP + 2 - OFF - 1 - rows]
    out_ref[:, 0 : OFF + 1, :] = jnp.where(position == 1, low, 0.0)
    out_ref[:, OFF + 1 : OFF + 1 + rows, :] = own
    out_ref[:, OFF + 1 + rows : YP + 2, :] = jnp.where(position == 0, high, 0.0)


def forward_kernel(
    lines, rows_y, field_ref, k1_ref, k2_ref, k3_ref,
    rate_ref, pre1_ref, pre2_ref, h1_ref, h2_ref, taps_ref,
    d9, w1, w2, w3, h1b, h2, z9, cells,
):
    l2, l1 = lines + 4, lines + 2
    fill_thin_band(k1_ref[...], w1, False)
    fill_wide_band(k2_ref[...], w2)
    fill_thin_band(k3_ref[...], w3, True)
    fill_taps(field_ref, d9, l2)
    taps_ref[...] = d9[2 : 2 + lines].reshape(lines * YP, 9 * NZ).astype(BF16)
    clear_pads(h1b)

    @pl.loop(0, GROUPS)
    def _(g):
        lanes = pl.ds(pl.multiple_of(g * GROUP, 128), GROUP)
        taps = d9[...].reshape(l2 * YP, 9 * NZ).astype(BF16)
        pre = jnp.dot(taps, w1[:, lanes], preferred_element_type=F32)
        pre = pre.reshape(l2, YP, GROUP)
        pre1_ref[:, :, lanes] = pre[2 : 2 + lines]
        inside, _ = y_masks(rows_y, l2, GROUP)
        _, owned = y_masks(rows_y, lines, GROUP)
        value = jnp.where(inside, pre * sigmoid(pre), 0.0)
        h1_ref[:, :, lanes] = jnp.where(owned, value[2 : 2 + lines], 0.0).astype(BF16)
        store_shifted(h1b, g, value)

    @pl.loop(0, GROUPS)
    def _(g):
        lanes = pl.ds(pl.multiple_of(g * GROUP, 128), GROUP)
        pre = wide_conv(h1b, w2, g, l1).reshape(l1, YP, GROUP)
        pre2_ref[:, :, lanes] = pre
        inside, _ = y_masks(rows_y, l1, GROUP)
        _, owned = y_masks(rows_y, lines, GROUP)
        value = jnp.where(inside, pre * sigmoid(pre), 0.0)
        h2[:, :, lanes] = value.astype(BF16)
        h2_ref[:, :, lanes] = jnp.where(owned, value[1 : 1 + lines], 0.0).astype(BF16)

    z9[...] = lax.dot_general(
        h2[...].reshape(l1 * YP, LANES), w3[...], NT, preferred_element_type=F32
    ).reshape(l1, YP, 9 * NZ)
    total = jnp.zeros((lines, rows_y, NZ), F32)
    for ab in range(9):
        a, b = ab // 3, ab % 3
        row = OFF - 1 + b
        total = total + z9[a : a + lines, row : row + rows_y, ab * NZ : (ab + 1) * NZ]
    cells[...] = jnp.exp(total).reshape(lines * rows_y, NZ)
    groups = lines * rows_y // 8
    for tile in range(3):
        parts = [
            cells[pl.ds(j, groups, stride=8), :][:, start : start + length]
            for j, at, _, start, length in PIECES
            if at == tile
        ]
        rate_ref[pl.ds(tile, groups, stride=3), :] = jnp.concatenate(parts, axis=1)


def tile_kernel(
    total_cells, rate_ref, target_ref, count_ref, slot_ref, land_ref,
    red_ref, loss_ref, main_ref, side_ref,
    msg, recv, back, ret, marks, grad, main, side,
    send_sem, recv_sem, send_back, recv_back, send_halo, recv_halo,
):
    tiles = rate_ref.shape[0]
    me, other = lax.axis_index("los"), lax.axis_index("tr")
    size = lax.axis_size("los")

    def peer(distance):
        return (lax.rem(me + distance + size, size), other)

    distances = [d for d in range(SPREAD) if d != REACH]
    barrier = pltpu.get_barrier_semaphore()
    for d in distances:
        pl.semaphore_signal(barrier, inc=1, device_id=peer(d - REACH), device_id_type=MESH)
    across = [(lax.rem(me + k + size, size), 1 - other) for k in (-1, 0, 1)]
    for device in across:
        pl.semaphore_signal(barrier, inc=1, device_id=device, device_id_type=MESH)

    def add_tile(t, perm):
        hit = iota((128, 128), 0) == target_ref[pl.ds(t, 1), :]
        column = jnp.sum(jnp.where(hit, rate_ref[pl.ds(t, 1), :], 0.0), axis=1, keepdims=True)
        return jnp.where(iota((128, tiles), 1) == t, column, perm)

    perm = lax.fori_loop(0, tiles, add_tile, jnp.zeros((128, tiles), F32), unroll=4)
    pick = jnp.where(iota((SLOTS, tiles), 0) == slot_ref[...], 1.0, 0.0)
    sent = lax.dot_general(pick, perm, NT, precision=HIGH, preferred_element_type=F32)
    sent = sent.reshape(SPREAD, PITCH, 128)
    landing = land_ref[...].reshape(SPREAD, 1, 128)
    msg[...] = jnp.where(iota((SPREAD, PITCH, 128), 1) == CAP, landing, sent)

    pl.semaphore_wait(barrier, len(distances) + 3)
    copies = []
    for d in distances:
        copy = pltpu.make_async_remote_copy(
            src_ref=msg.at[d], dst_ref=recv.at[d],
            send_sem=send_sem.at[d], recv_sem=recv_sem.at[d],
            device_id=peer(d - REACH), device_id_type=MESH,
        )
        copy.start()
        copies.append(copy)
    recv[REACH] = msg[REACH]
    for copy in copies:
        copy.wait_recv()
    for d in range(SPREAD):
        marks[0:1, d * PITCH : (d + 1) * PITCH] = recv[d, CAP : CAP + 1, 0:PITCH]
    place = jnp.where(
        iota((tiles, SLOTS), 0).astype(F32) == marks[0:1, 0:SLOTS], 1.0, 0.0
    )
    arrived = jnp.dot(
        place, recv[...].reshape(SLOTS, 128), precision=HIGH, preferred_element_type=F32
    )
    rate = BACKGROUND + arrived
    red_ref[...] = rate
    counts = count_ref[...].astype(F32)
    lam = (1.0 - counts / rate) / total_cells
    back[...] = lax.dot_general(
        place, lam, TN, precision=HIGH, preferred_element_type=F32
    ).reshape(SPREAD, PITCH, 128)
    returns = []
    for d in distances:
        copy = pltpu.make_async_remote_copy(
            src_ref=back.at[d], dst_ref=ret.at[d],
            send_sem=send_back.at[d], recv_sem=recv_back.at[d],
            device_id=peer(REACH - d), device_id_type=MESH,
        )
        copy.start()
        returns.append(copy)
    ret[REACH] = back[REACH]
    loss_ref[...] = jnp.sum(rate - counts * jnp.log(rate), axis=0, keepdims=True) / total_cells
    for copy in returns:
        copy.wait_recv()
    moved = lax.dot_general(
        pick, ret[...].reshape(SLOTS, 128), TN, precision=HIGH, preferred_element_type=F32
    )
    picked = jnp.take_along_axis(moved, target_ref[...], axis=1)
    grad[...] = (picked * rate_ref[...]).astype(BF16).astype(F32)
    halo = []
    top = grad.at[tiles - EDGE : tiles]
    bottom = grad.at[0:EDGE]
    for n, (source, target, device) in enumerate([
        (top, main.at[0], peer(1)),
        (bottom, main.at[1], peer(-1)),
        (top, side.at[0:EDGE], across[2]),
        (bottom, side.at[EDGE + tiles : 2 * EDGE + tiles], across[0]),
        (grad, side.at[EDGE : EDGE + tiles], across[1]),
    ]):
        copy = pltpu.make_async_remote_copy(
            src_ref=source, dst_ref=target, send_sem=send_halo.at[n], recv_sem=recv_halo.at[n],
            device_id=device, device_id_type=MESH,
        )
        copy.start()
        halo.append(copy)
    main_ref[EDGE : EDGE + tiles, :] = grad[...]
    for copy in halo:
        copy.wait_recv()
    main_ref[0:EDGE, :] = main[0]
    main_ref[EDGE + tiles : 2 * EDGE + tiles, :] = main[1]
    side_ref[...] = side[...]
    for copy in copies + returns + halo:
        copy.wait_send()


def thin_extract(product, fold, turned):
    diff = iota((NZ, LANES), 0) - (iota((NZ, LANES), 1) >> 5)
    rows = []
    for ab in range(9):
        block = product[ab * NZ : (ab + 1) * NZ, :]
        for c in range(3):
            rows.append(
                jnp.sum(jnp.where(diff == c - 1, block, 0.0), axis=0, keepdims=True)
            )
    rows = rows[::-1] if turned else rows
    rows = jnp.concatenate(rows + [jnp.zeros((5, LANES), F32)], axis=0)
    return jnp.dot(rows, fold, precision=HIGH, preferred_element_type=F32)


def fold_matrix(width):
    return jnp.where((iota((width, HID), 0) & (HID - 1)) == iota((width, HID), 1), 1.0, 0.0)


def backward_kernel(
    lines, rows_y, main_ref, side_ref, pre1_ref, pre2_ref, h1_ref, h2_ref, taps_ref, k2_ref, k3_ref,
    out_ref,
    g9, w2, w3, a2b, a1, h1t, prod, sums, cells, wide,
):
    l1 = lines + 2
    fill_wide_band(k2_ref[...], w2)
    fill_thin_band(k3_ref[...], w3, False)
    l2 = lines + 4
    groups = l2 * rows_y // 8
    skip = EDGE - 6 * rows_y // 8
    for source, source_ref in enumerate((main_ref, side_ref)):
        for j in range(8):
            parts = [
                source_ref[pl.ds(skip + tile, groups, stride=3), :][:, first : first + length]
                for at, tile, first, _, length in PIECES
                if at == j
            ]
            row = parts[0] if len(parts) == 1 else jnp.concatenate(parts, axis=1)
            cells[source, pl.ds(j, groups, stride=8), :] = row
    own = cells[0].reshape(l2, rows_y, NZ)
    other = cells[1].reshape(l2, rows_y, NZ)
    join_rows(wide, own, other[:, :8], other[:, rows_y - 8 :])
    fill_taps(wide, g9, l1)
    clear_pads(a2b)

    @pl.loop(0, GROUPS)
    def _(g):
        lanes = pl.ds(pl.multiple_of(g * GROUP, 128), GROUP)
        taps = g9[...].reshape(l1 * YP, 9 * NZ).astype(BF16)
        grad = jnp.dot(taps, w3[:, lanes], preferred_element_type=F32)
        grad = grad.reshape(l1, YP, GROUP) * slope(pre2_ref[:, :, lanes])
        inside, _ = y_masks(rows_y, l1, GROUP)
        store_shifted(a2b, g, jnp.where(inside, grad, 0.0))
        h1t[g] = h1_ref[:, :, lanes].reshape(lines * YP, GROUP).astype(F32).T.astype(BF16)

    @pl.loop(0, GROUPS)
    def _(g):
        lanes = pl.ds(pl.multiple_of(g * GROUP, 128), GROUP)
        grad = wide_conv(a2b, w2, g, lines).reshape(lines, YP, GROUP)
        grad = grad * slope(pre1_ref[:, :, lanes])
        _, owned = y_masks(rows_y, lines, GROUP)
        a1[:, :, lanes] = jnp.where(owned, grad, 0.0).astype(BF16)

    fold = fold_matrix(LANES)
    prod[...] = lax.dot_general(
        taps_ref[...], a1[...].reshape(lines * YP, LANES), TN, preferred_element_type=F32
    )
    out_ref[27 * HID : 28 * HID, :] = thin_extract(prod, fold, False)
    prod[...] = lax.dot_general(
        g9[1 : 1 + lines].reshape(lines * YP, 9 * NZ).astype(BF16),
        h2_ref[...].reshape(lines * YP, LANES), TN, preferred_element_type=F32,
    )
    out_ref[28 * HID : 29 * HID, :] = thin_extract(prod, fold, True)

    lane_z = iota((HID, 2 * GROUP), 1) >> 5
    for ab in range(9):
        a, b = ab // 3, ab % 3
        total = jnp.zeros((GROUP, 2 * GROUP), F32)
        for g in range(GROUPS):
            block = a2b[b, a : a + lines, :, g * GROUP : (g + 2) * GROUP]
            total = total + jnp.dot(
                h1t[g], block.reshape(lines * YP, 2 * GROUP), preferred_element_type=F32
            )
        for c in range(3):
            part = jnp.zeros((HID, 2 * GROUP), F32)
            for z in range(8):
                part = jnp.where(lane_z == z + 3 + c, total[z * HID : (z + 1) * HID, :], part)
            row = (26 - 3 * ab - c) * HID
            sums[row : row + HID, :] = part
    out_ref[0 : 27 * HID, :] = jnp.dot(
        sums[...], fold_matrix(2 * GROUP), precision=HIGH, preferred_element_type=F32
    )


def halo_kernel(
    lines, rows_y, width, own_ref, out_ref, stage, low, high, side, side_low, side_high,
    send_sem, recv_sem,
):
    me, other = lax.axis_index("los"), lax.axis_index("tr")
    size = lax.axis_size("los")
    up, down = lax.rem(me + 1, size), lax.rem(me + size - 1, size)
    barrier = pltpu.get_barrier_semaphore()
    devices = [(up, other), (down, other), (me, 1 - other), (up, 1 - other), (down, 1 - other)]
    for device in devices:
        pl.semaphore_signal(barrier, inc=1, device_id=device, device_id_type=MESH)
    own = own_ref[...].reshape(lines, rows_y, NZ)
    stage[...] = jnp.where(other == 0, own[:, rows_y - 8 :], own[:, :8])
    pl.semaphore_wait(barrier, len(devices))
    parts = [
        (own_ref.at[(lines - width) * rows_y : lines * rows_y], low),
        (own_ref.at[0 : width * rows_y], high),
        (stage, side),
        (stage.at[lines - width : lines], side_low),
        (stage.at[0:width], side_high),
    ]
    copies = []
    for n, (source, target) in enumerate(parts):
        copy = pltpu.make_async_remote_copy(
            src_ref=source, dst_ref=target, send_sem=send_sem.at[n], recv_sem=recv_sem.at[n],
            device_id=devices[n], device_id_type=MESH,
        )
        copy.start()
        copies.append(copy)
    for copy in copies:
        copy.wait_recv()
    near, far = low[...].reshape(width, rows_y, NZ), high[...].reshape(width, rows_y, NZ)
    join_rows(out_ref.at[0:width], near, side_low[...], side_low[...])
    join_rows(out_ref.at[width : width + lines], own, side[...], side[...])
    join_rows(out_ref.at[width + lines : 2 * width + lines], far, side_high[...], side_high[...])
    for copy in copies:
        copy.wait_send()


def sum_kernel(
    in_ref, loss_ref, out_ref, total_ref, mine, parts, pairs, done,
    send_one, recv_one, send_two, recv_two, send_three, recv_three,
):
    me, other = lax.axis_index("los"), lax.axis_index("tr")
    blocks = lax.axis_size("los") // SHARDS
    block, shard = me // SHARDS, lax.rem(me, SHARDS)
    barrier = pltpu.get_barrier_semaphore()
    group = [
        (block * SHARDS + lax.rem(shard + k, SHARDS), other) for k in range(1, SHARDS)
    ]
    count = 2 * blocks
    index = block * 2 + other
    column = []
    for k in range(1, count):
        peer = lax.rem(index + k, count)
        column.append(((peer // 2) * SHARDS + shard, lax.rem(peer, 2)))
    for device in group + column:
        pl.semaphore_signal(barrier, inc=1, device_id=device, device_id_type=MESH)
    for q in range(4):
        mine[0:PACK, q * HID : (q + 1) * HID] = in_ref[q * PACK : (q + 1) * PACK, :]
    rest = SHARDS * SHARD - PACK
    mine[PACK : SHARDS * SHARD, :] = jnp.where(iota((rest, 128), 0) == 0, loss_ref[...], 0.0)
    pl.semaphore_wait(barrier, len(group) + len(column))

    def rows(k):
        start = lax.rem(shard + k, SHARDS) * SHARD
        return pl.ds(pl.multiple_of(start, SHARD), SHARD)

    copies = []

    def send(source, target, sends, recvs, n, device):
        copy = pltpu.make_async_remote_copy(
            src_ref=source, dst_ref=target, send_sem=sends.at[n], recv_sem=recvs.at[n],
            device_id=device, device_id_type=MESH,
        )
        copy.start()
        copies.append(copy)
        return copy

    first = [
        send(mine.at[rows(k)], parts.at[k], send_one, recv_one, k, group[k - 1])
        for k in range(1, SHARDS)
    ]
    total = mine[rows(0), :]
    for k in range(1, SHARDS):
        first[k - 1].wait_recv()
        total = total + parts[k]
    parts[0] = total
    second = [
        send(parts.at[0], pairs.at[index], send_two, recv_two, k, column[k - 1])
        for k in range(1, count)
    ]
    pairs[index] = total
    for copy in second:
        copy.wait_recv()
    total = pairs[0]
    for k in range(1, count):
        total = total + pairs[k]
    done[rows(0), :] = total
    third = [
        send(done.at[rows(0)], done.at[rows(0)], send_three, recv_three, k, group[k - 1])
        for k in range(1, SHARDS)
    ]
    for copy in third:
        copy.wait_recv()
    for q in range(4):
        out_ref[q * PACK : (q + 1) * PACK, :] = done[0:PACK, q * HID : (q + 1) * HID]
    total_ref[...] = jnp.sum(done[PACK : PACK + 1, :], axis=1, keepdims=True)
    for copy in copies:
        copy.wait_send()


def on_device(
    density, observed_counts, cell_targets, shift_bins, kernel_first, kernel_second, kernel_third
):
    lines, width_tiles = shift_bins.shape
    plane = density.shape[1]
    rows_y = plane // NZ
    tiles = lines * width_tiles
    total_cells = lines * lax.axis_size("los") * plane * lax.axis_size("tr")
    l1, l2 = lines + 2, lines + 4
    vmem = pl.BlockSpec(memory_space=pltpu.VMEM)
    third = kernel_third.reshape(27, HID)
    second_back = kernel_second.reshape(27, HID, HID)[::-1].transpose(0, 2, 1).reshape(-1, HID)

    line = jnp.arange(lines, dtype=jnp.int32)[:, None]
    tile = jnp.arange(width_tiles, dtype=jnp.int32)[None, :]
    reach_line = line + shift_bins
    step = jnp.floor_divide(reach_line, lines)
    landing = ((reach_line - step * lines) * width_tiles + tile).reshape(-1)
    step = (step + REACH).reshape(-1)
    order = jnp.arange(tiles)
    earlier = (step[:, None] == step[None, :]) & (order[:, None] < order[None, :])
    rank = jnp.sum(earlier.astype(jnp.int32), axis=0)
    slot = step * PITCH + rank
    marks = jnp.sum(
        jnp.where(slot[:, None] == jnp.arange(SLOTS)[None, :], landing[:, None] + 1, 0), axis=0
    ) - 1
    marks = jnp.pad(
        marks.astype(F32).reshape(SPREAD, PITCH), ((0, 0), (0, 128 - PITCH)), constant_values=-1.0
    )

    five = pltpu.SemaphoreType.DMA((5,))
    corner = pltpu.VMEM((3, 8, NZ), F32)
    field = pl.pallas_call(
        functools.partial(halo_kernel, lines, rows_y, 3),
        out_shape=jax.ShapeDtypeStruct((lines + 6, YP + 2, NZ), F32),
        in_specs=[vmem],
        out_specs=vmem,
        scratch_shapes=[
            pltpu.VMEM((lines, 8, NZ), F32),
            pltpu.VMEM((3 * rows_y, NZ), F32),
            pltpu.VMEM((3 * rows_y, NZ), F32),
            pltpu.VMEM((lines, 8, NZ), F32),
            corner, corner, five, five,
        ],
        compiler_params=pltpu.CompilerParams(collective_id=1, has_side_effects=True),
        name="halo",
    )(density.astype(F32).reshape(lines * rows_y, NZ))
    rate, pre1, pre2, h1, h2, taps = pl.pallas_call(
        functools.partial(forward_kernel, lines, rows_y),
        out_shape=[
            jax.ShapeDtypeStruct((tiles, 128), F32),
            jax.ShapeDtypeStruct((lines, YP, LANES), F32),
            jax.ShapeDtypeStruct((l1, YP, LANES), F32),
            jax.ShapeDtypeStruct((lines, YP, LANES), BF16),
            jax.ShapeDtypeStruct((lines, YP, LANES), BF16),
            jax.ShapeDtypeStruct((lines * YP, 9 * NZ), BF16),
        ],
        in_specs=[vmem] * 4,
        out_specs=[vmem] * 6,
        scratch_shapes=[
            pltpu.VMEM((l2, YP, 9 * NZ), F32),
            pltpu.VMEM((9 * NZ, LANES), BF16),
            pltpu.VMEM((9, 2 * GROUP, GROUP), BF16),
            pltpu.VMEM((9 * NZ, LANES), BF16),
            pltpu.VMEM((3, l2, YP, WIDE), BF16),
            pltpu.VMEM((l1, YP, LANES), BF16),
            pltpu.VMEM((l1, YP, 9 * NZ), F32),
            pltpu.VMEM((lines * rows_y, NZ), F32),
        ],
        compiler_params=pltpu.CompilerParams(vmem_limit_bytes=LIMIT),
        name="forward",
    )(field, kernel_first, kernel_second, third)

    box = pltpu.VMEM((SPREAD, PITCH, 128), F32)
    sems = pltpu.SemaphoreType.DMA((SPREAD,))
    redshift_rate, loss_part, grad_main, grad_side = pl.pallas_call(
        functools.partial(tile_kernel, total_cells),
        out_shape=[
            jax.ShapeDtypeStruct((tiles, 128), F32),
            jax.ShapeDtypeStruct((1, 128), F32),
            jax.ShapeDtypeStruct((tiles + 2 * EDGE, 128), F32),
            jax.ShapeDtypeStruct((tiles + 2 * EDGE, 128), F32),
        ],
        in_specs=[vmem] * 5,
        out_specs=[vmem] * 4,
        scratch_shapes=[
            box, box, box, box,
            pltpu.VMEM((8, 512), F32),
            pltpu.VMEM((tiles, 128), F32),
            pltpu.VMEM((2, EDGE, 128), F32),
            pltpu.VMEM((tiles + 2 * EDGE, 128), F32),
            sems, sems, sems, sems, five, five,
        ],
        compiler_params=pltpu.CompilerParams(
            vmem_limit_bytes=LIMIT, collective_id=0, has_side_effects=True
        ),
        name="tiles",
    )(
        rate,
        cell_targets.reshape(tiles, 128),
        observed_counts.reshape(tiles, 128),
        slot.reshape(1, tiles),
        marks,
    )

    packed = pl.pallas_call(
        functools.partial(backward_kernel, lines, rows_y),
        out_shape=jax.ShapeDtypeStruct((29 * HID, HID), F32),
        in_specs=[vmem] * 9,
        out_specs=vmem,
        scratch_shapes=[
            pltpu.VMEM((l1, YP, 9 * NZ), F32),
            pltpu.VMEM((9, 2 * GROUP, GROUP), BF16),
            pltpu.VMEM((9 * NZ, LANES), BF16),
            pltpu.VMEM((3, l1, YP, WIDE), BF16),
            pltpu.VMEM((lines, YP, LANES), BF16),
            pltpu.VMEM((GROUPS, GROUP, lines * YP), BF16),
            pltpu.VMEM((9 * NZ, LANES), F32),
            pltpu.VMEM((27 * HID, 2 * GROUP), F32),
            pltpu.VMEM((2, l2 * rows_y, NZ), F32),
            pltpu.VMEM((l2, YP + 2, NZ), F32),
        ],
        compiler_params=pltpu.CompilerParams(vmem_limit_bytes=LIMIT),
        name="backward",
    )(grad_main, grad_side, pre1, pre2, h1, h2, taps, second_back, third[::-1])
    blocks = lax.axis_size("los") // SHARDS
    piece = pltpu.SemaphoreType.DMA((SHARDS,))
    pair = pltpu.SemaphoreType.DMA((2 * blocks,))
    packed, loss = pl.pallas_call(
        sum_kernel,
        out_shape=[
            jax.ShapeDtypeStruct((29 * HID, HID), F32),
            jax.ShapeDtypeStruct((1, 1), F32),
        ],
        in_specs=[vmem] * 2,
        out_specs=[vmem] * 2,
        scratch_shapes=[
            pltpu.VMEM((SHARDS * SHARD, 128), F32),
            pltpu.VMEM((SHARDS, SHARD, 128), F32),
            pltpu.VMEM((2 * blocks, SHARD, 128), F32),
            pltpu.VMEM((SHARDS * SHARD, 128), F32),
            piece, piece, pair, pair, piece, piece,
        ],
        compiler_params=pltpu.CompilerParams(collective_id=2, has_side_effects=True),
        name="sum",
    )(packed, loss_part)
    return (
        redshift_rate.reshape(lines, plane),
        loss.reshape(()),
        packed[27 * HID : 27 * HID + 27],
        packed[: 27 * HID],
        packed[28 * HID : 28 * HID + 27].reshape(27 * HID, 1),
    )


def solution(mesh):
    return jax.shard_map(
        on_device,
        mesh=mesh,
        in_specs=(P("los", "tr"), P("los", "tr"), P("los", "tr"), P("los", "tr"), P(), P(), P()),
        out_specs=(P("los", "tr"), P(), P(), P(), P()),
        check_vma=False,
    )
```

```python
import functools

import jax
import jax.numpy as jnp
from jax import lax
from jax.experimental import pallas as pl
from jax.experimental.pallas import tpu as pltpu
from jax.sharding import PartitionSpec as P

NZ = 48
REACH = 6
SPREAD = 2 * REACH + 1
CAP = 24
EDGE = 24
SHARDS = 16
SHARD = 16
PITCH = 32
SLOTS = SPREAD * PITCH
HID = 32
PACK = 29 * HID // 4
YP = 32
OFF = 4
LANES = NZ * HID
PAD = 128
WIDE = LANES + 2 * PAD
GROUP = 256
GROUPS = LANES // GROUP
BACKGROUND = 0.2
MESH = pl.DeviceIdType.MESH
HIGH = lax.Precision.HIGHEST
LIMIT = 56 * 1024 * 1024
F32 = jnp.float32
BF16 = jnp.bfloat16
NT = (((1,), (1,)), ((), ()))
TN = (((0,), (0,)), ((), ()))


def row_pieces():
    pieces = []
    for j in range(8):
        done = 0
        while done < NZ:
            tile, first = divmod(j * NZ + done, 128)
            length = min(NZ - done, 128 - first)
            pieces.append((j, tile, first, done, length))
            done += length
    return pieces


PIECES = row_pieces()


def iota(shape, dim):
    return lax.broadcasted_iota(jnp.int32, shape, dim)


def repeat_lanes(kernel, width):
    rep = jnp.where((iota((HID, width), 1) & (HID - 1)) == iota((HID, width), 0), 1.0, 0.0)
    return jnp.dot(kernel, rep.astype(BF16), preferred_element_type=F32)


def fill_thin_band(kernel, out_ref, flip, turned=False):
    tiled = repeat_lanes(kernel, LANES)
    diff = iota((NZ, LANES), 0) - (iota((NZ, LANES), 1) >> 5)
    if flip:
        diff = -diff
    for ab in range(9):
        block = jnp.zeros((NZ, LANES), F32)
        for c in range(3):
            row = 26 - 3 * ab - c if turned else 3 * ab + c
            block = jnp.where(diff == c - 1, tiled[row : row + 1, :], block)
        out_ref[ab * NZ : (ab + 1) * NZ, :] = block.astype(BF16)


def fill_wide_band(kernel, out_ref):
    tiled = repeat_lanes(kernel, GROUP)
    zo = iota((HID, GROUP), 1) >> 5
    for ab in range(9):
        for zi in range(16):
            block = jnp.zeros((HID, GROUP), F32)
            for c in range(3):
                if 0 <= zi - 3 - c < 8:
                    row = (3 * ab + c) * HID
                    block = jnp.where(zo == zi - 3 - c, tiled[row : row + HID, :], block)
            out_ref[ab, zi * HID : (zi + 1) * HID, :] = block.astype(BF16)


def fill_taps(src_ref, out_ref, lines):
    for ab in range(9):
        a, b = ab // 3, ab % 3
        out_ref[:, :, ab * NZ : (ab + 1) * NZ] = src_ref[a : a + lines, b : b + YP, :]


def y_masks(rows_y, lines, width):
    index = iota((lines, YP, width), 1) - OFF
    start = lax.axis_index("tr") * rows_y
    total = lax.axis_size("tr") * rows_y
    inside = (index + start >= 0) & (index + start < total)
    owned = (index >= 0) & (index < rows_y)
    return inside, owned


def sigmoid(v):
    return 1.0 / (1.0 + jnp.exp(-v))


def slope(v):
    s = sigmoid(v)
    return s * (1.0 + v * (1.0 - s))


def store_shifted(out_ref, g, value):
    lanes = pl.ds(pl.multiple_of(PAD + g * GROUP, 128), GROUP)
    out_ref[0, :, :, lanes] = pltpu.roll(value, 1, 1).astype(BF16)
    out_ref[1, :, :, lanes] = value.astype(BF16)
    out_ref[2, :, :, lanes] = pltpu.roll(value, YP - 1, 1).astype(BF16)


def clear_pads(out_ref):
    shape = out_ref.shape[:-1] + (PAD,)
    out_ref[:, :, :, 0:PAD] = jnp.zeros(shape, BF16)
    out_ref[:, :, :, WIDE - PAD : WIDE] = jnp.zeros(shape, BF16)


def wide_conv(src_ref, band_ref, g, lines):
    total = jnp.zeros((lines * YP, GROUP), F32)
    lanes = pl.ds(pl.multiple_of(g * GROUP, 128), 2 * GROUP)
    for ab in range(9):
        a, b = ab // 3, ab % 3
        block = src_ref[b, a : a + lines, :, lanes].reshape(lines * YP, 2 * GROUP)
        total = total + jnp.dot(block, band_ref[ab], preferred_element_type=F32)
    return total


def join_rows(out_ref, own, after, before):
    rows = own.shape[1]
    position = lax.axis_index("tr")
    low = before[:, 8 - OFF - 1 :]
    high = after[:, : YP + 2 - OFF - 1 - rows]
    out_ref[:, 0 : OFF + 1, :] = jnp.where(position == 1, low, 0.0)
    out_ref[:, OFF + 1 : OFF + 1 + rows, :] = own
    out_ref[:, OFF + 1 + rows : YP + 2, :] = jnp.where(position == 0, high, 0.0)


def forward_kernel(
    lines, rows_y, field_ref, k1_ref, k2_ref, k3_ref,
    rate_ref, pre1_ref, pre2_ref, h1_ref, h2_ref, taps_ref,
    d9, w1, w2, w3, h1b, h2, z9, cells,
):
    l2, l1 = lines + 4, lines + 2
    fill_thin_band(k1_ref[...], w1, False)
    fill_wide_band(k2_ref[...], w2)
    fill_thin_band(k3_ref[...], w3, True)
    fill_taps(field_ref, d9, l2)
    taps_ref[...] = d9[2 : 2 + lines].reshape(lines * YP, 9 * NZ).astype(BF16)
    clear_pads(h1b)

    @pl.loop(0, GROUPS)
    def _(g):
        lanes = pl.ds(pl.multiple_of(g * GROUP, 128), GROUP)
        taps = d9[...].reshape(l2 * YP, 9 * NZ).astype(BF16)
        pre = jnp.dot(taps, w1[:, lanes], preferred_element_type=F32)
        pre = pre.reshape(l2, YP, GROUP)
        pre1_ref[:, :, lanes] = pre[2 : 2 + lines]
        inside, _ = y_masks(rows_y, l2, GROUP)
        _, owned = y_masks(rows_y, lines, GROUP)
        value = jnp.where(inside, pre * sigmoid(pre), 0.0)
        h1_ref[:, :, lanes] = jnp.where(owned, value[2 : 2 + lines], 0.0).astype(BF16)
        store_shifted(h1b, g, value)

    @pl.loop(0, GROUPS)
    def _(g):
        lanes = pl.ds(pl.multiple_of(g * GROUP, 128), GROUP)
        pre = wide_conv(h1b, w2, g, l1).reshape(l1, YP, GROUP)
        pre2_ref[:, :, lanes] = pre
        inside, _ = y_masks(rows_y, l1, GROUP)
        _, owned = y_masks(rows_y, lines, GROUP)
        value = jnp.where(inside, pre * sigmoid(pre), 0.0)
        h2[:, :, lanes] = value.astype(BF16)
        h2_ref[:, :, lanes] = jnp.where(owned, value[1 : 1 + lines], 0.0).astype(BF16)

    z9[...] = lax.dot_general(
        h2[...].reshape(l1 * YP, LANES), w3[...], NT, preferred_element_type=F32
    ).reshape(l1, YP, 9 * NZ)
    total = jnp.zeros((lines, rows_y, NZ), F32)
    for ab in range(9):
        a, b = ab // 3, ab % 3
        row = OFF - 1 + b
        total = total + z9[a : a + lines, row : row + rows_y, ab * NZ : (ab + 1) * NZ]
    cells[...] = jnp.exp(total).reshape(lines * rows_y, NZ)
    groups = lines * rows_y // 8
    for tile in range(3):
        parts = [
            cells[pl.ds(j, groups, stride=8), :][:, start : start + length]
            for j, at, _, start, length in PIECES
            if at == tile
        ]
        rate_ref[pl.ds(tile, groups, stride=3), :] = jnp.concatenate(parts, axis=1)


def tile_kernel(
    total_cells, rate_ref, target_ref, count_ref, slot_ref, land_ref,
    red_ref, loss_ref, main_ref, side_ref,
    msg, recv, back, ret, marks, grad, main, side,
    send_sem, recv_sem, send_back, recv_back, send_halo, recv_halo,
):
    tiles = rate_ref.shape[0]
    me, other = lax.axis_index("los"), lax.axis_index("tr")
    size = lax.axis_size("los")

    def peer(distance):
        return (lax.rem(me + distance + size, size), other)

    distances = [d for d in range(SPREAD) if d != REACH]
    barrier = pltpu.get_barrier_semaphore()
    for d in distances:
        pl.semaphore_signal(barrier, inc=1, device_id=peer(d - REACH), device_id_type=MESH)
    across = [(lax.rem(me + k + size, size), 1 - other) for k in (-1, 0, 1)]
    for device in across:
        pl.semaphore_signal(barrier, inc=1, device_id=device, device_id_type=MESH)

    def add_tile(t, perm):
        hit = iota((128, 128), 0) == target_ref[pl.ds(t, 1), :]
        column = jnp.sum(jnp.where(hit, rate_ref[pl.ds(t, 1), :], 0.0), axis=1, keepdims=True)
        return jnp.where(iota((128, tiles), 1) == t, column, perm)

    perm = lax.fori_loop(0, tiles, add_tile, jnp.zeros((128, tiles), F32), unroll=4)
    pick = jnp.where(iota((SLOTS, tiles), 0) == slot_ref[...], 1.0, 0.0)
    sent = lax.dot_general(pick, perm, NT, precision=HIGH, preferred_element_type=F32)
    sent = sent.reshape(SPREAD, PITCH, 128)
    landing = land_ref[...].reshape(SPREAD, 1, 128)
    msg[...] = jnp.where(iota((SPREAD, PITCH, 128), 1) == CAP, landing, sent)

    pl.semaphore_wait(barrier, len(distances) + 3)
    copies = []
    for d in distances:
        copy = pltpu.make_async_remote_copy(
            src_ref=msg.at[d], dst_ref=recv.at[d],
            send_sem=send_sem.at[d], recv_sem=recv_sem.at[d],
            device_id=peer(d - REACH), device_id_type=MESH,
        )
        copy.start()
        copies.append(copy)
    recv[REACH] = msg[REACH]
    for copy in copies:
        copy.wait_recv()
    for d in range(SPREAD):
        marks[0:1, d * PITCH : (d + 1) * PITCH] = recv[d, CAP : CAP + 1, 0:PITCH]
    place = jnp.where(
        iota((tiles, SLOTS), 0).astype(F32) == marks[0:1, 0:SLOTS], 1.0, 0.0
    )
    arrived = jnp.dot(
        place, recv[...].reshape(SLOTS, 128), precision=HIGH, preferred_element_type=F32
    )
    rate = BACKGROUND + arrived
    red_ref[...] = rate
    counts = count_ref[...].astype(F32)
    lam = (1.0 - counts / rate) / total_cells
    back[...] = lax.dot_general(
        place, lam, TN, precision=HIGH, preferred_element_type=F32
    ).reshape(SPREAD, PITCH, 128)
    returns = []
    for d in distances:
        copy = pltpu.make_async_remote_copy(
            src_ref=back.at[d], dst_ref=ret.at[d],
            send_sem=send_back.at[d], recv_sem=recv_back.at[d],
            device_id=peer(REACH - d), device_id_type=MESH,
        )
        copy.start()
        returns.append(copy)
    ret[REACH] = back[REACH]
    loss_ref[...] = jnp.sum(rate - counts * jnp.log(rate), axis=0, keepdims=True) / total_cells
    for copy in returns:
        copy.wait_recv()
    moved = lax.dot_general(
        pick, ret[...].reshape(SLOTS, 128), TN, precision=HIGH, preferred_element_type=F32
    )
    picked = jnp.take_along_axis(moved, target_ref[...], axis=1)
    grad[...] = (picked * rate_ref[...]).astype(BF16).astype(F32)
    halo = []
    top = grad.at[tiles - EDGE : tiles]
    bottom = grad.at[0:EDGE]
    for n, (source, target, device) in enumerate([
        (top, main.at[0], peer(1)),
        (bottom, main.at[1], peer(-1)),
        (top, side.at[0:EDGE], across[2]),
        (bottom, side.at[EDGE + tiles : 2 * EDGE + tiles], across[0]),
        (grad, side.at[EDGE : EDGE + tiles], across[1]),
    ]):
        copy = pltpu.make_async_remote_copy(
            src_ref=source, dst_ref=target, send_sem=send_halo.at[n], recv_sem=recv_halo.at[n],
            device_id=device, device_id_type=MESH,
        )
        copy.start()
        halo.append(copy)
    main_ref[EDGE : EDGE + tiles, :] = grad[...]
    for copy in halo:
        copy.wait_recv()
    main_ref[0:EDGE, :] = main[0]
    main_ref[EDGE + tiles : 2 * EDGE + tiles, :] = main[1]
    side_ref[...] = side[...]
    for copy in copies + returns + halo:
        copy.wait_send()


def thin_extract(product, fold, turned):
    diff = iota((NZ, LANES), 0) - (iota((NZ, LANES), 1) >> 5)
    rows = []
    for ab in range(9):
        block = product[ab * NZ : (ab + 1) * NZ, :]
        for c in range(3):
            rows.append(
                jnp.sum(jnp.where(diff == c - 1, block, 0.0), axis=0, keepdims=True)
            )
    rows = rows[::-1] if turned else rows
    rows = jnp.concatenate(rows + [jnp.zeros((5, LANES), F32)], axis=0)
    return jnp.dot(rows, fold, precision=HIGH, preferred_element_type=F32)


def fold_matrix(width):
    return jnp.where((iota((width, HID), 0) & (HID - 1)) == iota((width, HID), 1), 1.0, 0.0)


def backward_kernel(
    lines, rows_y, main_ref, side_ref, pre1_ref, pre2_ref, h1_ref, h2_ref, taps_ref, k2_ref, k3_ref,
    out_ref,
    g9, w2, w3, a2b, a1, h1t, prod, sums, cells, wide,
):
    l1 = lines + 2
    fill_wide_band(k2_ref[...], w2)
    fill_thin_band(k3_ref[...], w3, False, True)
    l2 = lines + 4
    groups = l2 * rows_y // 8
    skip = EDGE - 6 * rows_y // 8
    for source, source_ref in enumerate((main_ref, side_ref)):
        for j in range(8):
            parts = [
                source_ref[pl.ds(skip + tile, groups, stride=3), :][:, first : first + length]
                for at, tile, first, _, length in PIECES
                if at == j
            ]
            row = parts[0] if len(parts) == 1 else jnp.concatenate(parts, axis=1)
            cells[source, pl.ds(j, groups, stride=8), :] = row
    own = cells[0].reshape(l2, rows_y, NZ)
    other = cells[1].reshape(l2, rows_y, NZ)
    join_rows(wide, own, other[:, :8], other[:, rows_y - 8 :])
    fill_taps(wide, g9, l1)
    clear_pads(a2b)

    @pl.loop(0, GROUPS)
    def _(g):
        lanes = pl.ds(pl.multiple_of(g * GROUP, 128), GROUP)
        taps = g9[...].reshape(l1 * YP, 9 * NZ).astype(BF16)
        grad = jnp.dot(taps, w3[:, lanes], preferred_element_type=F32)
        grad = grad.reshape(l1, YP, GROUP) * slope(pre2_ref[:, :, lanes])
        inside, _ = y_masks(rows_y, l1, GROUP)
        store_shifted(a2b, g, jnp.where(inside, grad, 0.0))
        h1t[g] = h1_ref[:, :, lanes].reshape(lines * YP, GROUP).astype(F32).T.astype(BF16)

    @pl.loop(0, GROUPS)
    def _(g):
        lanes = pl.ds(pl.multiple_of(g * GROUP, 128), GROUP)
        grad = wide_conv(a2b, w2, g, lines).reshape(lines, YP, GROUP)
        grad = grad * slope(pre1_ref[:, :, lanes])
        _, owned = y_masks(rows_y, lines, GROUP)
        a1[:, :, lanes] = jnp.where(owned, grad, 0.0).astype(BF16)

    fold = fold_matrix(LANES)
    prod[...] = lax.dot_general(
        taps_ref[...], a1[...].reshape(lines * YP, LANES), TN, preferred_element_type=F32
    )
    out_ref[27 * HID : 28 * HID, :] = thin_extract(prod, fold, False)
    prod[...] = lax.dot_general(
        g9[1 : 1 + lines].reshape(lines * YP, 9 * NZ).astype(BF16),
        h2_ref[...].reshape(lines * YP, LANES), TN, preferred_element_type=F32,
    )
    out_ref[28 * HID : 29 * HID, :] = thin_extract(prod, fold, True)

    lane_z = iota((HID, 2 * GROUP), 1) >> 5
    for ab in range(9):
        a, b = ab // 3, ab % 3
        total = jnp.zeros((GROUP, 2 * GROUP), F32)
        for g in range(GROUPS):
            block = a2b[b, a : a + lines, :, g * GROUP : (g + 2) * GROUP]
            total = total + jnp.dot(
                h1t[g], block.reshape(lines * YP, 2 * GROUP), preferred_element_type=F32
            )
        for c in range(3):
            part = jnp.zeros((HID, 2 * GROUP), F32)
            for z in range(8):
                part = jnp.where(lane_z == z + 3 + c, total[z * HID : (z + 1) * HID, :], part)
            row = (26 - 3 * ab - c) * HID
            sums[row : row + HID, :] = part
    out_ref[0 : 27 * HID, :] = jnp.dot(
        sums[...], fold_matrix(2 * GROUP), precision=HIGH, preferred_element_type=F32
    )


def halo_kernel(
    lines, rows_y, width, own_ref, out_ref, stage, low, high, side, side_low, side_high,
    send_sem, recv_sem,
):
    me, other = lax.axis_index("los"), lax.axis_index("tr")
    size = lax.axis_size("los")
    up, down = lax.rem(me + 1, size), lax.rem(me + size - 1, size)
    barrier = pltpu.get_barrier_semaphore()
    devices = [(up, other), (down, other), (me, 1 - other), (up, 1 - other), (down, 1 - other)]
    for device in devices:
        pl.semaphore_signal(barrier, inc=1, device_id=device, device_id_type=MESH)
    own = own_ref[...].reshape(lines, rows_y, NZ)
    stage[...] = jnp.where(other == 0, own[:, rows_y - 8 :], own[:, :8])
    pl.semaphore_wait(barrier, len(devices))
    parts = [
        (own_ref.at[(lines - width) * rows_y : lines * rows_y], low),
        (own_ref.at[0 : width * rows_y], high),
        (stage, side),
        (stage.at[lines - width : lines], side_low),
        (stage.at[0:width], side_high),
    ]
    copies = []
    for n, (source, target) in enumerate(parts):
        copy = pltpu.make_async_remote_copy(
            src_ref=source, dst_ref=target, send_sem=send_sem.at[n], recv_sem=recv_sem.at[n],
            device_id=devices[n], device_id_type=MESH,
        )
        copy.start()
        copies.append(copy)
    for copy in copies:
        copy.wait_recv()
    near, far = low[...].reshape(width, rows_y, NZ), high[...].reshape(width, rows_y, NZ)
    join_rows(out_ref.at[0:width], near, side_low[...], side_low[...])
    join_rows(out_ref.at[width : width + lines], own, side[...], side[...])
    join_rows(out_ref.at[width + lines : 2 * width + lines], far, side_high[...], side_high[...])
    for copy in copies:
        copy.wait_send()


def sum_kernel(
    in_ref, loss_ref, first_ref, second_ref, third_ref, total_ref, out_ref, mine, parts, pairs, done,
    send_one, recv_one, send_two, recv_two, send_three, recv_three,
):
    me, other = lax.axis_index("los"), lax.axis_index("tr")
    blocks = lax.axis_size("los") // SHARDS
    block, shard = me // SHARDS, lax.rem(me, SHARDS)
    barrier = pltpu.get_barrier_semaphore()
    group = [
        (block * SHARDS + lax.rem(shard + k, SHARDS), other) for k in range(1, SHARDS)
    ]
    count = 2 * blocks
    index = block * 2 + other
    column = []
    for k in range(1, count):
        peer = lax.rem(index + k, count)
        column.append(((peer // 2) * SHARDS + shard, lax.rem(peer, 2)))
    for device in group + column:
        pl.semaphore_signal(barrier, inc=1, device_id=device, device_id_type=MESH)
    for q in range(4):
        mine[0:PACK, q * HID : (q + 1) * HID] = in_ref[q * PACK : (q + 1) * PACK, :]
    rest = SHARDS * SHARD - PACK
    mine[PACK : SHARDS * SHARD, :] = jnp.where(iota((rest, 128), 0) == 0, loss_ref[...], 0.0)
    pl.semaphore_wait(barrier, len(group) + len(column))

    def rows(k):
        start = lax.rem(shard + k, SHARDS) * SHARD
        return pl.ds(pl.multiple_of(start, SHARD), SHARD)

    copies = []

    def send(source, target, sends, recvs, n, device):
        copy = pltpu.make_async_remote_copy(
            src_ref=source, dst_ref=target, send_sem=sends.at[n], recv_sem=recvs.at[n],
            device_id=device, device_id_type=MESH,
        )
        copy.start()
        copies.append(copy)
        return copy

    first = [
        send(mine.at[rows(k)], parts.at[k], send_one, recv_one, k, group[k - 1])
        for k in range(1, SHARDS)
    ]
    total = mine[rows(0), :]
    for k in range(1, SHARDS):
        first[k - 1].wait_recv()
        total = total + parts[k]
    parts[0] = total
    second = [
        send(parts.at[0], pairs.at[index], send_two, recv_two, k, column[k - 1])
        for k in range(1, count)
    ]
    pairs[index] = total
    for copy in second:
        copy.wait_recv()
    total = pairs[0]
    for k in range(1, count):
        total = total + pairs[k]
    done[rows(0), :] = total
    third = [
        send(done.at[rows(0)], done.at[rows(0)], send_three, recv_three, k, group[k - 1])
        for k in range(1, SHARDS)
    ]
    for copy in third:
        copy.wait_recv()
    for q in range(4):
        out_ref[q * PACK : (q + 1) * PACK, :] = done[0:PACK, q * HID : (q + 1) * HID]
    second_ref[...] = out_ref[0 : 27 * HID, :]
    first_ref[...] = out_ref[27 * HID : 27 * HID + 27, :]
    third_ref[...] = out_ref[28 * HID : 28 * HID + 27, :]
    total_ref[...] = jnp.sum(done[PACK : PACK + 1, :], axis=1, keepdims=True)
    for copy in copies:
        copy.wait_send()


def on_device(
    density, observed_counts, cell_targets, shift_bins, kernel_first, kernel_second, kernel_third
):
    lines, width_tiles = shift_bins.shape
    plane = density.shape[1]
    rows_y = plane // NZ
    tiles = lines * width_tiles
    total_cells = lines * lax.axis_size("los") * plane * lax.axis_size("tr")
    l1, l2 = lines + 2, lines + 4
    vmem = pl.BlockSpec(memory_space=pltpu.VMEM)
    third = kernel_third.reshape(27, HID)
    second_back = kernel_second.reshape(27, HID, HID)[::-1].transpose(0, 2, 1).reshape(-1, HID)

    line = jnp.arange(lines, dtype=jnp.int32)[:, None]
    tile = jnp.arange(width_tiles, dtype=jnp.int32)[None, :]
    reach_line = line + shift_bins
    step = jnp.floor_divide(reach_line, lines)
    landing = ((reach_line - step * lines) * width_tiles + tile).reshape(-1)
    step = (step + REACH).reshape(-1)
    order = jnp.arange(tiles)
    earlier = (step[:, None] == step[None, :]) & (order[:, None] < order[None, :])
    rank = jnp.sum(earlier.astype(jnp.int32), axis=0)
    slot = step * PITCH + rank
    marks = jnp.sum(
        jnp.where(slot[:, None] == jnp.arange(SLOTS)[None, :], landing[:, None] + 1, 0), axis=0
    ) - 1
    marks = jnp.pad(
        marks.astype(F32).reshape(SPREAD, PITCH), ((0, 0), (0, 128 - PITCH)), constant_values=-1.0
    )

    five = pltpu.SemaphoreType.DMA((5,))
    corner = pltpu.VMEM((3, 8, NZ), F32)
    field = pl.pallas_call(
        functools.partial(halo_kernel, lines, rows_y, 3),
        out_shape=jax.ShapeDtypeStruct((lines + 6, YP + 2, NZ), F32),
        in_specs=[vmem],
        out_specs=vmem,
        scratch_shapes=[
            pltpu.VMEM((lines, 8, NZ), F32),
            pltpu.VMEM((3 * rows_y, NZ), F32),
            pltpu.VMEM((3 * rows_y, NZ), F32),
            pltpu.VMEM((lines, 8, NZ), F32),
            corner, corner, five, five,
        ],
        compiler_params=pltpu.CompilerParams(collective_id=1, has_side_effects=True),
        name="halo",
    )(density.astype(F32).reshape(lines * rows_y, NZ))
    rate, pre1, pre2, h1, h2, taps = pl.pallas_call(
        functools.partial(forward_kernel, lines, rows_y),
        out_shape=[
            jax.ShapeDtypeStruct((tiles, 128), F32),
            jax.ShapeDtypeStruct((lines, YP, LANES), F32),
            jax.ShapeDtypeStruct((l1, YP, LANES), F32),
            jax.ShapeDtypeStruct((lines, YP, LANES), BF16),
            jax.ShapeDtypeStruct((lines, YP, LANES), BF16),
            jax.ShapeDtypeStruct((lines * YP, 9 * NZ), BF16),
        ],
        in_specs=[vmem] * 4,
        out_specs=[vmem] * 6,
        scratch_shapes=[
            pltpu.VMEM((l2, YP, 9 * NZ), F32),
            pltpu.VMEM((9 * NZ, LANES), BF16),
            pltpu.VMEM((9, 2 * GROUP, GROUP), BF16),
            pltpu.VMEM((9 * NZ, LANES), BF16),
            pltpu.VMEM((3, l2, YP, WIDE), BF16),
            pltpu.VMEM((l1, YP, LANES), BF16),
            pltpu.VMEM((l1, YP, 9 * NZ), F32),
            pltpu.VMEM((lines * rows_y, NZ), F32),
        ],
        compiler_params=pltpu.CompilerParams(vmem_limit_bytes=LIMIT),
        name="forward",
    )(field, kernel_first, kernel_second, third)

    box = pltpu.VMEM((SPREAD, PITCH, 128), F32)
    sems = pltpu.SemaphoreType.DMA((SPREAD,))
    redshift_rate, loss_part, grad_main, grad_side = pl.pallas_call(
        functools.partial(tile_kernel, total_cells),
        out_shape=[
            jax.ShapeDtypeStruct((tiles, 128), F32),
            jax.ShapeDtypeStruct((1, 128), F32),
            jax.ShapeDtypeStruct((tiles + 2 * EDGE, 128), F32),
            jax.ShapeDtypeStruct((tiles + 2 * EDGE, 128), F32),
        ],
        in_specs=[vmem] * 5,
        out_specs=[vmem] * 4,
        scratch_shapes=[
            box, box, box, box,
            pltpu.VMEM((8, 512), F32),
            pltpu.VMEM((tiles, 128), F32),
            pltpu.VMEM((2, EDGE, 128), F32),
            pltpu.VMEM((tiles + 2 * EDGE, 128), F32),
            sems, sems, sems, sems, five, five,
        ],
        compiler_params=pltpu.CompilerParams(
            vmem_limit_bytes=LIMIT, collective_id=0, has_side_effects=True
        ),
        name="tiles",
    )(
        rate,
        cell_targets.reshape(tiles, 128),
        observed_counts.reshape(tiles, 128),
        slot.reshape(1, tiles),
        marks,
    )

    packed = pl.pallas_call(
        functools.partial(backward_kernel, lines, rows_y),
        out_shape=jax.ShapeDtypeStruct((29 * HID, HID), F32),
        in_specs=[vmem] * 9,
        out_specs=vmem,
        scratch_shapes=[
            pltpu.VMEM((l1, YP, 9 * NZ), F32),
            pltpu.VMEM((9, 2 * GROUP, GROUP), BF16),
            pltpu.VMEM((9 * NZ, LANES), BF16),
            pltpu.VMEM((3, l1, YP, WIDE), BF16),
            pltpu.VMEM((lines, YP, LANES), BF16),
            pltpu.VMEM((GROUPS, GROUP, lines * YP), BF16),
            pltpu.VMEM((9 * NZ, LANES), F32),
            pltpu.VMEM((27 * HID, 2 * GROUP), F32),
            pltpu.VMEM((2, l2 * rows_y, NZ), F32),
            pltpu.VMEM((l2, YP + 2, NZ), F32),
        ],
        compiler_params=pltpu.CompilerParams(vmem_limit_bytes=LIMIT),
        name="backward",
    )(grad_main, grad_side, pre1, pre2, h1, h2, taps, second_back, third)
    blocks = lax.axis_size("los") // SHARDS
    piece = pltpu.SemaphoreType.DMA((SHARDS,))
    pair = pltpu.SemaphoreType.DMA((2 * blocks,))
    grad_first, grad_second, grad_third, loss = pl.pallas_call(
        sum_kernel,
        out_shape=[
            jax.ShapeDtypeStruct((27, HID), F32),
            jax.ShapeDtypeStruct((27 * HID, HID), F32),
            jax.ShapeDtypeStruct((27, HID), F32),
            jax.ShapeDtypeStruct((1, 1), F32),
        ],
        in_specs=[vmem] * 2,
        out_specs=[vmem] * 4,
        scratch_shapes=[
            pltpu.VMEM((29 * HID, HID), F32),
            pltpu.VMEM((SHARDS * SHARD, 128), F32),
            pltpu.VMEM((SHARDS, SHARD, 128), F32),
            pltpu.VMEM((2 * blocks, SHARD, 128), F32),
            pltpu.VMEM((SHARDS * SHARD, 128), F32),
            piece, piece, pair, pair, piece, piece,
        ],
        compiler_params=pltpu.CompilerParams(collective_id=2, has_side_effects=True),
        name="sum",
    )(packed, loss_part)
    return (
        redshift_rate.reshape(lines, plane),
        loss.reshape(()),
        grad_first,
        grad_second,
        grad_third.reshape(27 * HID, 1),
    )


def solution(mesh):
    return jax.shard_map(
        on_device,
        mesh=mesh,
        in_specs=(P("los", "tr"), P("los", "tr"), P("los", "tr"), P("los", "tr"), P(), P(), P()),
        out_specs=(P("los", "tr"), P(), P(), P(), P()),
        check_vma=False,
    )
```
